256 devices in a mesh: ctx: 64 (over z, y_hi, x), tp: 4 (over y_lo, core).
Axes of the slice: x: 4, y: 4 (y_hi: 2, y_lo: 2; y = y_hi * 2 + y_lo), z: 8, core: 2. Of those that a mesh axis runs over, the one named last changes fastest.
Arguments:
- queries: bfloat16 [8192, 8192], P('ctx', 'tp'), may hold values from -68 to 68
- keys: bfloat16 [8192, 512], P('ctx', 'tp'), may hold values from -6 to 6
- values: bfloat16 [8192, 512], P('ctx', 'tp'), may hold values from -6 to 6
- pair_of: int32 [64], replicated, may hold values from 0 to 63, each once
- doc_start: int32 [1], replicated, may hold values from 2048 to 6144
- scored: int32 [128], P('ctx'), may hold values from 0 to 127
- targets: int32 [128], P('ctx'), may hold values from 0 to 64127
- residual_rows: bfloat16 [128, 16384], P(None, 'ctx'), may hold values from -9 to 9
- out_weight: bfloat16 [8192, 16384], P('tp', 'ctx'), may hold values from -0.1875 to 0.1875
- norm_gain: bfloat16 [16384], P('ctx'), may hold values from 0.25 to 1.75
- head_weight: bfloat16 [16384, 64128], P('ctx', 'tp'), may hold values from -1 to 1
Outputs:
- attended: bfloat16 [8192, 8192], P('ctx', 'tp')
- log_prob: float32 [128], P('ctx')
The draws below stay inside these ranges and needn't reach their ends.
Inputs may be any that keep to these rules, and one draw needn't show every extreme that they name: Device d holds sequence blocks pair_of[d] and 2 * 64 - 1 - pair_of[d], each of 64 tokens; every value once.
All inputs are finite; a program needn't handle non-finite values.
Results may differ from the reference program's by a relative error of at most 0.0075.
Values may be sent and summed in bfloat16 or wider, within the bound.
No kernel may reach another device: no remote copies, remote signals or barrier semaphores. Data moves between devices by JAX's collectives and lax.ppermute only.
A program may use at most 192 MiB of HBM per device.

```python
import math
import jax
import jax.numpy as jnp
from jax import lax

D = 16384
HD = 128
HEADS = 64
KVH = 4
TOK_DEV = 128
R_DEV = 2
GROUP = 16
SEQ = 8192
R = 128
VOCAB = 64128
N_CTX = 64


def dominant_columns(key, target_low, target_high):
    first_cols = jax.random.randint(jax.random.fold_in(key, 201), (R,), 0, VOCAB)
    second_cols = jax.random.randint(jax.random.fold_in(key, 202), (R,), 0, VOCAB)
    half_signs = (jax.random.randint(jax.random.fold_in(key, 203), (R, D // 2), 0, 2) * 2 - 1).astype(jnp.float32)
    pattern = jnp.concatenate([half_signs, -half_signs], axis=1)
    order = jax.random.permutation(jax.random.fold_in(key, 204), D)
    pattern = pattern[:, order]
    target = jnp.exp(jax.random.uniform(jax.random.fold_in(key, 205), (R,), jnp.float32, jnp.log(jnp.float32(target_low)), jnp.log(jnp.float32(target_high))))
    offset = jax.random.uniform(jax.random.fold_in(key, 206), (R,), jnp.float32, 1.0, 3.0)
    return (first_cols, second_cols, pattern, target, offset)


def draw_keys(key, part):
    key = jax.random.fold_in(key, 3)
    drawn = jnp.clip(jax.random.normal(key, (SEQ, KVH * HD), jnp.float32), -6.0, 6.0)
    return drawn.astype(jnp.bfloat16)


def draw_queries(key, part):
    key = jax.random.fold_in(key, 4)
    drawn = jnp.clip(jax.random.normal(key, (SEQ, HEADS, HD), jnp.float32), -6.0, 6.0)
    return drawn.reshape(SEQ, HEADS * HD).astype(jnp.bfloat16)


def draw_residual_rows(key, part):
    target_low, target_high = (3.0, 8.0)
    first_cols, second_cols, pattern, target, offset = dominant_columns(key, target_low, target_high)
    key = jax.random.fold_in(key, 5)
    drawn = jnp.clip(jax.random.normal(key, (R, D), jnp.float32), -6.0, 6.0)
    return jnp.clip(drawn + pattern, -9.0, 9.0).astype(jnp.bfloat16)


def draw_head_weight(key, part):
    amplitude, target_low, target_high = (1.0, 3.0, 8.0)
    first_cols, second_cols, pattern, target, offset = dominant_columns(key, target_low, target_high)
    key = jax.random.fold_in(key, 9)
    width_scale = 3.0 / jnp.sqrt(jnp.float32(D))
    column_scale = jnp.exp(jax.random.uniform(jax.random.fold_in(key, 4), (1, VOCAB), jnp.float32, -0.51, 0.53))
    base = jnp.clip(jax.random.normal(key, (D, VOCAB), jnp.float32), -6.0, 6.0)
    noise = base * column_scale * width_scale
    first_lift = jnp.minimum(target * 2.5 / (amplitude * D), 0.5)
    second_lift = first_lift * (1.0 - offset / target)
    noise = noise.at[:, first_cols].add(pattern.T * first_lift[None, :])
    noise = noise.at[:, second_cols].add(pattern.T * second_lift[None, :])
    return jnp.clip(noise, -1.0, 1.0).astype(jnp.bfloat16)


def touch_ends(drawn, key, low, largest):
    spot = [jax.random.randint(jax.random.fold_in(key, axis), (), 0, length) for axis, length in enumerate(drawn.shape)]
    main_axis = drawn.shape.index(max(drawn.shape))
    beside = spot[:main_axis] + [(spot[main_axis] + 1) % drawn.shape[main_axis]] + spot[main_axis + 1:]
    return drawn.at[tuple(spot)].set(low).at[tuple(beside)].set(largest)


def level_of(own_key, dims, split, least, high):
    gain = 1.0
    for position, parts in split:
        heights = jax.random.uniform(jax.random.fold_in(jax.random.fold_in(own_key, 6), position), (parts,), jnp.float32, least / len(split), high / len(split))
        gain = gain * jnp.repeat(jnp.exp(heights), dims[position] // parts).reshape((-1,) + (1,) * (len(dims) - 1 - position))
    return gain


def centred(own_key, dims, scale, most, shards=(), kind=jnp.bfloat16):
    entries = scale * jax.random.normal(own_key, dims, jnp.float32)
    if shards:
        entries = entries * level_of(own_key, dims, shards, -0.22, 0.18)
    return jnp.clip(entries, -most, most).astype(kind)


def setup_inputs(seed: int = 0) -> dict:
    arg_keys = jax.random.split(jax.random.key(seed), 12)
    queries = draw_queries(jax.random.fold_in(arg_keys[11], 71), 0)
    keys = draw_keys(jax.random.fold_in(arg_keys[11], 71), 0)
    values = centred(arg_keys[2], (SEQ, KVH * HD), 1.0, 6.0, ((0, 64), (1, 4)))
    pair_of = jax.random.permutation(arg_keys[3], N_CTX).astype(jnp.int32)
    doc_start = jax.random.randint(arg_keys[4], (1,), SEQ // 4, 3 * SEQ // 4 + 1).astype(jnp.int32)
    scored = touch_ends(jax.random.randint(arg_keys[5], (R,), 0, TOK_DEV), jax.random.fold_in(arg_keys[5], 1), 0, TOK_DEV - 1).astype(jnp.int32)
    targets = touch_ends(jax.random.randint(arg_keys[6], (R,), 0, VOCAB), jax.random.fold_in(arg_keys[6], 1), 0, VOCAB - 1).astype(jnp.int32)
    residual_rows = draw_residual_rows(jax.random.fold_in(arg_keys[11], 71), 0)
    out_weight = centred(arg_keys[8], (HEADS * HD, D), (HEADS * HD // 9) ** -0.5, 0.1875, ((0, 4), (1, 64)))
    norm_gain = jnp.clip(1.0 + 0.15 * jax.random.normal(arg_keys[9], (D,), jnp.float32), 0.25, 1.75).astype(jnp.bfloat16)
    head_weight = draw_head_weight(jax.random.fold_in(arg_keys[11], 71), 0)
    return dict(queries=queries, keys=keys, values=values, pair_of=pair_of, doc_start=doc_start, scored=scored, targets=targets, residual_rows=residual_rows, out_weight=out_weight, norm_gain=norm_gain, head_weight=head_weight)


NEG = -1e+30
EPS = 1e-05

def place_rows(row_index, pair_of, tok_dev):
    devices = pair_of.shape[0]
    owner_device = row_index // tok_dev
    inner_row = row_index % tok_dev
    half_rows = tok_dev // 2
    owner_pair = lax.optimization_barrier(jnp.sum(jnp.where(owner_device[:, None] == jnp.arange(devices, dtype=jnp.int32)[None, :], pair_of[None, :], 0), axis=1)).astype(jnp.int32)
    first_half = owner_pair * half_rows + inner_row
    second_half = (2 * devices - 1 - owner_pair) * half_rows + inner_row - half_rows
    return jnp.where(inner_row < half_rows, first_half, second_half).astype(jnp.int32)

def segment_of(positions, doc_start):
    return lax.optimization_barrier(jnp.sum((positions[:, None] >= doc_start[None, :]).astype(jnp.int32), axis=1)).astype(jnp.int32)

def reference(queries, keys, values, pair_of, doc_start, scored, targets, residual_rows, out_weight, norm_gain, head_weight):
    row_index = jnp.arange(SEQ, dtype=jnp.int32)
    positions = place_rows(row_index, pair_of, TOK_DEV)
    segments = segment_of(positions, doc_start)
    row_block = math.gcd(SEQ, 256)
    block_count = SEQ // row_block
    score_scale = 1.0 / math.sqrt(HD)
    query_all = queries.reshape(SEQ, KVH, GROUP, HD)
    key_all = keys.reshape(SEQ, KVH, HD).astype(jnp.float32)
    value_all = values.reshape(SEQ, KVH, HD).astype(jnp.float32)
    pos_blocks = positions.reshape(block_count, row_block)
    seg_blocks = segments.reshape(block_count, row_block)
    results = []
    for kv_head in range(KVH):
        key_rows = key_all[:, kv_head]
        value_rows = value_all[:, kv_head]

        def one_block(pieces):
            query_rows, query_pos, query_seg = pieces
            scores = jnp.einsum('tgd,sd->tgs', query_rows.astype(jnp.float32), key_rows) * score_scale
            visible = (positions[None, :] <= query_pos[:, None]) & (segments[None, :] == query_seg[:, None])
            visible = visible[:, None, :]
            scores = jnp.where(visible, scores, NEG)
            row_peak = lax.optimization_barrier(jnp.max(scores, axis=2, keepdims=True))
            weights = jnp.where(visible, jnp.exp(scores - row_peak), 0.0)
            row_total = lax.optimization_barrier(jnp.sum(weights, axis=2, keepdims=True))
            rounded = lax.optimization_barrier(weights.astype(jnp.bfloat16)).astype(jnp.float32)
            return jnp.einsum('tgs,sd->tgd', rounded, value_rows) / row_total
        query_blocks = query_all[:, kv_head].reshape(block_count, row_block, GROUP, HD)
        outcome = lax.map(one_block, (query_blocks, pos_blocks, seg_blocks))
        results.append(outcome.reshape(SEQ, GROUP, HD))
    attended = jnp.stack(results, axis=1).reshape(SEQ, HEADS * HD).astype(jnp.bfloat16)
    owners = jnp.arange(R, dtype=jnp.int32) // R_DEV
    chosen_rows = (owners * TOK_DEV + scored).astype(jnp.int32)
    selected = jnp.take(attended, chosen_rows, axis=0)
    mixed = jnp.dot(selected, out_weight, preferred_element_type=jnp.float32)
    hidden = (mixed + residual_rows.astype(jnp.float32)).astype(jnp.bfloat16)
    hidden_f = hidden.astype(jnp.float32)
    inverse = lax.rsqrt(lax.optimization_barrier(jnp.mean(hidden_f * hidden_f, axis=1)) + EPS)
    scaled = (hidden_f * norm_gain.astype(jnp.float32)[None, :]).astype(jnp.bfloat16)
    logits = jnp.dot(scaled, head_weight, preferred_element_type=jnp.float32) * inverse[:, None]
    row_peak = lax.optimization_barrier(jnp.max(logits, axis=1))
    log_total = jnp.log(lax.optimization_barrier(jnp.sum(jnp.exp(logits - row_peak[:, None]), axis=1)))
    picked = jnp.take_along_axis(logits, targets[:, None].astype(jnp.int32), axis=1)[:, 0]
    log_prob = picked - (row_peak + log_total)
    return (attended, log_prob)
```

```python
import functools
import math

import jax
import jax.numpy as jnp
import numpy as np
from jax import lax
from jax.experimental import pallas as pl
from jax.experimental.pallas import tpu as pltpu
from jax.sharding import PartitionSpec as P

D = 16384
HD = 128
EPS = 1e-05
NEG = -1e30
SCALE = math.log2(math.e) / math.sqrt(HD)
BIG = 16
NX, NY, NZ = 4, 2, 8
EVEN = (0, 2, 4, 6)
NEAR = ((0, 0), (2, 0), (0, 1), (2, 1))
HALF = 64
TILE = 1024
ROWS = 256
HEAD_TILE = 1152


def inner_spread(x):
    count = lax.axis_size("ctx")
    groups = [[o * BIG + i for i in range(BIG)] for o in range(count // BIG)]
    return lax.all_to_all(x, "ctx", 0, 0, axis_index_groups=groups, tiled=True)


def shifted(block, dx, dy, dz):
    pairs = []
    for i in range(lax.axis_size("ctx")):
        z, y, x = i // (NX * NY), i // NX % NY, i % NX
        to = ((z + dz) % NZ * NY + (y + dy) % NY) * NX + (x + dx) % NX
        pairs.append((i, to))
    return lax.ppermute(block, "ctx", pairs)


def pinned(*arrays):
    return [pltpu.with_memory_space_constraint(x, pltpu.HBM) for x in arrays]


def tp_parts(x):
    return [x] + [lax.ppermute(x, "tp", [(i, i ^ k) for i in range(4)]) for k in (1, 2, 3)]


def nt_dot(a, b):
    return lax.dot_general(a, b, (((1,), (1,)), ((), ())), preferred_element_type=jnp.float32)


def pack_kernel(scored_ref, k_ref, v_ref, q_ref, out_ref, near_ref, sem):
    tok = k_ref.shape[0]
    r_dev = scored_ref.shape[0]
    wide = 2 * HD
    parts = q_ref.shape[1] // wide
    block = out_ref.shape[0]
    reads = []
    for j in range(r_dev):
        start = pl.multiple_of(scored_ref[j] // 16 * 16, 16)
        reads.append(
            pltpu.make_async_copy(q_ref.at[pl.ds(start, 16), :], near_ref.at[j], sem.at[j])
        )
    for i, ref in enumerate((k_ref, v_ref)):
        to = out_ref.at[pl.ds(0, tok), pl.ds(i * HD, HD)]
        reads.append(pltpu.make_async_copy(ref, to, sem.at[r_dev + i]))
    for read in reads:
        read.start()
    at = lax.broadcasted_iota(jnp.int32, (16, q_ref.shape[1]), 0)
    mark_row = lax.broadcasted_iota(jnp.int32, (16, wide), 0)
    marks = jnp.zeros((16, wide), jnp.int32)
    lines = []
    for j in range(r_dev):
        row = scored_ref[j]
        reads[j].wait()
        near = near_ref[j].astype(jnp.float32)
        line = jnp.sum(jnp.where(at == row % 16, near, 0.0), axis=0, keepdims=True)
        lines += [line[:, c * wide : (c + 1) * wide] for c in range(parts)]
        marks = jnp.where(mark_row == j, row, marks)
    out_ref[tok : block - 16, :] = jnp.concatenate(lines, axis=0).astype(jnp.bfloat16)
    out_ref[block - 16 :, :] = marks.astype(jnp.float32).astype(jnp.bfloat16)
    for read in reads[r_dev:]:
        read.wait()


def assembled(arrays, plans, size, name):
    count = len(arrays)

    def kernel(*refs):
        for plan, out in zip(plans, refs[count:]):
            for d, (i, b) in enumerate(plan):
                out[d * size : (d + 1) * size, :] = refs[i][b * size : (b + 1) * size, :]

    width = arrays[0].shape[1]
    vmem = pl.BlockSpec(memory_space=pltpu.VMEM)
    return pl.pallas_call(
        kernel,
        out_shape=[
            jax.ShapeDtypeStruct((len(plan) * size, width), arrays[0].dtype) for plan in plans
        ],
        in_specs=[vmem] * count,
        out_specs=[vmem] * len(plans),
        compiler_params=pltpu.CompilerParams(vmem_limit_bytes=8 << 20),
        name=name,
    )(*arrays)


def gathered(first, tok):
    even = assembled(first, [[(i, 0) for i in range(len(first))]], tok, "even")[0]
    near = [even] + [shifted(even, -dx, dy, 0) for dx, dy in NEAR[1:]]
    near_at = [[(dx, dy, dz, h) for dz in EVEN for h in range(2)] for dx, dy in NEAR]
    held = list(zip(near, near_at))

    def picked(held, want):
        return [(i, at.index(d)) for d in want for i, (_, at) in enumerate(held) if d in at]

    def moved(at, dx, dz):
        return [((x + dx) % NX, y, (z + dz) % NZ, h) for x, y, z, h in at]

    low_up = [(dx, dy, dz, 0) for dx, dy in NEAR for dz in (0, 2)]
    low_down = [(dx, dy, dz, 0) for dx, dy in NEAR for dz in (0, 6)]
    high = [(0, dy, dz, 1) for dy in range(NY) for dz in EVEN]
    sends = assembled(near, [picked(held, w) for w in (low_up, low_down, high)], HALF, "step_two")
    held += [
        (shifted(sends[0], 0, 0, -1), moved(low_up, 0, 1)),
        (shifted(sends[1], 0, 0, 1), moved(low_down, 0, -1)),
        (shifted(sends[2], -1, 0, 0), moved(high, 1, 0)),
        (shifted(sends[2], 1, 0, 0), moved(high, -1, 0)),
    ]
    low = [(0, dy, dz, 0) for dy in range(NY) for dz in range(NZ)]
    high_up = [(dx, dy, dz, 1) for dx in range(NX) for dy in range(NY) for dz in (0, 2)]
    high_down = [(dx, dy, dz, 1) for dx in range(NX) for dy in range(NY) for dz in (0, 6)]
    arrays = [array for array, _ in held]
    sends = assembled(arrays, [picked(held, w) for w in (low, high_up, high_down)], HALF, "step_one")
    held += [
        (shifted(sends[0], -1, 0, 0), moved(low, 1, 0)),
        (shifted(sends[0], 1, 0, 0), moved(low, -1, 0)),
        (shifted(sends[1], 0, 0, -1), moved(high_up, 0, 1)),
        (shifted(sends[2], 0, 0, 1), moved(high_down, 0, -1)),
    ]
    return held


def row_orders(r_dev):
    js = range(r_dev)
    ys = range(NY)
    p_keep = [
        (x, y, z, j) for zs in (EVEN, (1, 3), (7, 5)) for z in zs for x in (0, 2) for y in ys for j in js
    ]
    p_sent = [[(x, y, z, j) for z in (*EVEN, 1, 3, 7, 5) for y in ys for j in js] for x in (1, 3)]
    q_keep = [
        (x, y, z, j) for xs in ((0, 2), (1,), (3,)) for z in EVEN for x in xs for y in ys for j in js
    ]
    q_sent = [
        [(x, y, z, j) for z in zs for x in (0, 2, 1, 3) for y in ys for j in js]
        for zs in ((1, 3), (7, 5))
    ]
    return (p_keep, *p_sent), (q_keep, *q_sent)


def adding(out, kept, up, down, axis):
    def seen(rows, by):
        if axis == "x":
            return [((x + by) % NX, y, z, j) for x, y, z, j in rows]
        return [(x, y, (z + by) % NZ, j) for x, y, z, j in rows]

    rows = list(kept) + seen(up, -1) + seen(down, 1)
    return np.array([[float(a == b) for b in rows] for a in out], np.float32)


def scored_kernel(n_parts, table_ref, meta_ref, pos_ref, *refs):
    parts, kv, rest = refs[:n_parts], refs[n_parts:-7], refs[-7:]
    out_ref, k_out, v_out, k_ref, v_ref, s_ref, sem = rest
    n = 0
    for array in kv:
        for row in range(0, array.shape[0], HALF):
            to = pl.ds(pl.multiple_of(table_ref[n] * HALF, HALF), HALF)
            k_ref[to, :] = array[row : row + HALF, :HD]
            v_ref[to, :] = array[row : row + HALF, HD:]
            n += 1
    writes = [
        pltpu.make_async_copy(k_ref, k_out, sem.at[0]),
        pltpu.make_async_copy(v_ref, v_out, sem.at[1]),
    ]
    for write in writes:
        write.start()
    seq = k_ref.shape[0]
    rows = s_ref.shape[0]
    first = 2 * HALF
    doc = meta_ref[2]
    pos = jnp.concatenate([pos_ref[...]] * 2, axis=0)
    low = jnp.where(pos >= doc, doc, 0)
    q = jnp.concatenate(
        [
            part[first : part.shape[0] - 16, e * HD : (e + 1) * HD]
            for e in range(2)
            for part in parts
        ],
        axis=0,
    )
    step = 1024
    peak = jnp.full((rows, 1), NEG, jnp.float32)
    for t in range(0, seq, step):
        s = nt_dot(q, k_ref[t : t + step, :])
        at = t + lax.broadcasted_iota(jnp.int32, (rows, step), 1)
        s = jnp.where((at <= pos) & (at >= low), s, NEG)
        s_ref[:, t : t + step] = s
        peak = jnp.maximum(peak, jnp.max(s, axis=1, keepdims=True))
    total = jnp.zeros((rows, 1), jnp.float32)
    acc = jnp.zeros((rows, HD), jnp.float32)
    for t in range(0, seq, step):
        w = jnp.exp2((s_ref[:, t : t + step] - peak) * SCALE)
        total = total + jnp.sum(w, axis=1, keepdims=True)
        acc = acc + jnp.dot(
            w.astype(jnp.bfloat16), v_ref[t : t + step, :], preferred_element_type=jnp.float32
        )
    acc = (acc / total).astype(jnp.bfloat16)
    out_ref[...] = jnp.concatenate([acc[: rows // 2], acc[rows // 2 :]], axis=1)
    for write in writes:
        write.wait()


def main_kernel(side, meta_ref, q_ref, k_ref, v_ref, *refs):
    out_ref, buf_ref, k_buf, v_buf, qs_ref, m_ref, acc_ref, sem = refs[-8:]
    offset = side * buf_ref.shape[1]
    reads = []
    for c in range(2):
        for i, (ref, buf) in enumerate(((k_ref, k_buf), (v_ref, v_buf))):
            piece = pl.ds(c * (buf.shape[0] // 2), buf.shape[0] // 2)
            reads.append(
                pltpu.make_async_copy(ref.at[piece, :], buf.at[piece, :], sem.at[1 + 2 * c + i])
            )
            reads[-1].start()
    half = HALF
    heads = buf_ref.shape[1] // HD
    rows = heads * half
    doc = meta_ref[2]
    for b in range(2):
        for h in range(heads):
            columns = slice(offset + h * HD, offset + (h + 1) * HD)
            q = q_ref[b * half : (b + 1) * half, columns].astype(jnp.float32)
            q = q * SCALE
            high = q.astype(jnp.bfloat16)
            low = (q - high.astype(jnp.float32)).astype(jnp.bfloat16)
            qs_ref[h * half : (h + 1) * half, :] = jnp.concatenate([high, low], axis=1)
        first = meta_ref[b] * half
        m_ref[...] = jnp.full(m_ref.shape, NEG, jnp.float32)
        acc_ref[...] = jnp.zeros(acc_ref.shape, jnp.float32)
        begin = jnp.where(first >= doc, doc, 0)

        def tile(t, masked):
            base = pl.multiple_of(t * TILE, TILE)
            k = k_buf[pl.ds(base, TILE), :]
            k = jnp.concatenate([k, k], axis=1)
            v = v_buf[pl.ds(base, TILE), :]
            v = jnp.concatenate([v, jnp.ones_like(v)], axis=1)
            if masked:
                pos = first + lax.rem(lax.broadcasted_iota(jnp.int32, (ROWS, 1), 0), half)
                low = jnp.where(pos >= doc, doc, 0)
                at = base + lax.broadcasted_iota(jnp.int32, (ROWS, TILE), 1)
                visible = (at <= pos) & (at >= low)
            for r in range(0, rows, ROWS):
                span = slice(r, r + ROWS)
                s = nt_dot(qs_ref[span, :], k)
                if masked:
                    s = jnp.where(visible, s, NEG)
                old = m_ref[span, :]
                new = jnp.maximum(old, jnp.max(s, axis=1, keepdims=True))
                w = jnp.exp2(s - jnp.concatenate([new] * (TILE // HD), axis=1))
                if masked:
                    w = jnp.where(visible, w, 0.0)
                factor = jnp.exp2(old - new)
                m_ref[span, :] = new
                acc_ref[span, :] = acc_ref[span, :] * jnp.concatenate([factor] * 2, axis=1) + jnp.dot(
                    w.astype(jnp.bfloat16), v, preferred_element_type=jnp.float32
                )

        if b == 0:
            for read in reads:
                read.wait()

        def step(t, _):
            inside = (t * TILE >= begin) & (t * TILE + TILE - 1 <= first) & (
                (first >= doc) | (first + half <= doc)
            )

            @pl.when(inside)
            def _():
                tile(t, False)

            @pl.when(jnp.logical_not(inside))
            def _():
                tile(t, True)

            return 0

        lax.fori_loop(begin // TILE, (first + half - 1) // TILE + 1, step, 0)
        for h in range(heads):
            span = slice(h * half, (h + 1) * half)
            buf_ref[b * half : (b + 1) * half, h * HD : (h + 1) * HD] = (
                acc_ref[span, :HD] / acc_ref[span, HD:]
            ).astype(jnp.bfloat16)
    write = pltpu.make_async_copy(
        buf_ref, out_ref.at[:, pl.ds(offset, buf_ref.shape[1])], sem.at[0]
    )
    write.start()
    write.wait()


def project_kernel(rows_ref, w_ref, out_ref):
    out_ref[...] = jnp.dot(
        rows_ref[...], w_ref[...], preferred_element_type=jnp.float32
    ).astype(jnp.bfloat16)


def load_kernel(w_ref, out_ref, sem):
    vocab = w_ref.shape[0]
    reads = []
    for t in range(0, out_ref.shape[0], HEAD_TILE):
        piece = pl.ds(t, min(t + HEAD_TILE, vocab) - t)
        reads.append(
            pltpu.make_async_copy(w_ref.at[piece, :], out_ref.at[piece, :], sem.at[t // HEAD_TILE])
        )
        reads[-1].start()
    rest = (out_ref.shape[0] - vocab, out_ref.shape[1])
    out_ref[vocab:, :] = jnp.zeros(rest, out_ref.dtype)
    for read in reads:
        read.wait()


def head_kernel(vocab, p0, p1, p2, p3, res_ref, gain_ref, order_ref, w_ref, *outs):
    part = outs[0].shape[1]
    spans = [slice(t, t + HEAD_TILE) for t in range(0, 2 * part, HEAD_TILE)]
    f = lambda r: r[...].astype(jnp.float32)
    mixed = (f(p0) + f(p1)) + (f(p2) + f(p3))
    hidden = (mixed + f(res_ref)).astype(jnp.bfloat16).astype(jnp.float32)
    x = (hidden * f(gain_ref)).astype(jnp.bfloat16)
    square = jnp.sum(hidden * hidden, axis=1, keepdims=True)
    high = square.astype(jnp.bfloat16).astype(jnp.float32)
    lane = lax.broadcasted_iota(jnp.int32, (x.shape[0], HD), 1)
    terms = jnp.where(lane == 0, high, jnp.where(lane == 1, square - high, 0.0))
    source = lax.broadcasted_iota(jnp.int32, (x.shape[0], x.shape[0]), 1)
    moves = [(source == order_ref[:, c : c + 1]).astype(jnp.bfloat16) for c in range(2)]
    xs = [jnp.dot(m, x, preferred_element_type=jnp.float32).astype(jnp.bfloat16) for m in moves]
    terms = jnp.dot(moves[1], terms.astype(jnp.bfloat16), preferred_element_type=jnp.float32)
    for span in spans:
        side = span.start // part
        y = nt_dot(xs[side], w_ref[span, :])
        if span.stop > vocab:
            col = span.start + lax.broadcasted_iota(jnp.int32, y.shape, 1)
            y = jnp.where(
                col == vocab, terms[:, :1], jnp.where(col == vocab + 1, terms[:, 1:2], y)
            )
        y = y.astype(jnp.bfloat16)
        row = 0
        for out in outs[3 * side : 3 * side + 3]:
            to = slice(span.start - side * part, span.stop - side * part)
            out[:, to] = y[row : row + out.shape[0], :]
            row += out.shape[0]


def add_kernel(n_outs, n_ins, sides, *refs):
    for side in range(sides):
        matrix = refs[side]
        ins = refs[sides + side * n_ins : sides + (side + 1) * n_ins]
        outs = refs[sides + sides * n_ins :]
        shift = 0
        if len(outs) == n_outs:
            shift = side * ins[0].shape[1]
        else:
            outs = outs[side * n_outs : (side + 1) * n_outs]
        for c in range(0, ins[0].shape[1], HEAD_TILE):
            rows = jnp.concatenate([r[:, c : c + HEAD_TILE] for r in ins], axis=0)
            y = jnp.dot(matrix[...], rows, preferred_element_type=jnp.float32)
            row = 0
            for out in outs:
                out[:, shift + c : shift + c + HEAD_TILE] = y[row : row + out.shape[0], :].astype(
                    jnp.bfloat16
                )
                row += out.shape[0]


def added(matrices, sides, heights, joined, name):
    width = sides[0][0].shape[1]
    total = width * len(sides) if joined else width
    shapes = [jax.ShapeDtypeStruct((h, total), jnp.bfloat16) for h in heights]
    vmem = pl.BlockSpec(memory_space=pltpu.VMEM)
    ins = [jnp.asarray(m, jnp.bfloat16) for m in matrices] + [a for side in sides for a in side]
    outs = shapes if joined else shapes * len(sides)
    return pl.pallas_call(
        functools.partial(add_kernel, len(heights), len(sides[0]), len(sides)),
        out_shape=outs,
        in_specs=[vmem] * len(ins),
        out_specs=[vmem] * len(outs),
        compiler_params=pltpu.CompilerParams(vmem_limit_bytes=16 << 20),
        name=name,
    )(*ins)


def local(
    queries,
    keys,
    values,
    pair_of,
    doc_start,
    scored,
    targets,
    residual_rows,
    out_weight,
    norm_gain,
    head_weight,
):
    n_ctx = lax.axis_size("ctx")
    ctx = lax.axis_index("ctx")
    tp = lax.axis_index("tp")
    tok = queries.shape[0]
    half = tok // 2
    heads = queries.shape[1] // HD
    r_dev = scored.shape[0]
    vocab = head_weight.shape[1]
    vmem = pl.BlockSpec(memory_space=pltpu.VMEM)
    smem = pl.BlockSpec(memory_space=pltpu.SMEM)

    hbm = pl.BlockSpec(memory_space=pltpu.HBM)
    n_outer = n_ctx // BIG
    tokens = n_outer * r_dev
    seq = tok * n_ctx
    z, y, x = ctx // (NX * NY), ctx // NX % NY, ctx % NX
    owner = (ctx // BIG + jnp.arange(n_outer, dtype=jnp.int32)) % n_outer

    def pair_at(dx, dy, dz):
        place = [np.asarray(d, np.int32) for d in (dx, dy, dz)]
        at = ((z + place[2]) % NZ * NY + (y + place[1]) % NY) * NX + (x + place[0]) % NX
        every = jnp.arange(n_ctx, dtype=jnp.int32)
        return jnp.sum(jnp.where(at[:, None] == every[None, :], pair_of[None, :], 0), axis=1)

    def owned(x):
        return jnp.concatenate(
            [lax.dynamic_slice_in_dim(x, owner[k], 1, 0) for k in range(n_outer)], axis=0
        )

    block = tok + r_dev * heads // 2 + 16
    sent = pl.pallas_call(
        pack_kernel,
        out_shape=jax.ShapeDtypeStruct((block, 2 * HD), jnp.bfloat16),
        in_specs=[smem, hbm, hbm, hbm],
        out_specs=vmem,
        scratch_shapes=[
            pltpu.VMEM((r_dev, 16, heads * HD), jnp.bfloat16),
            pltpu.SemaphoreType.DMA((r_dev + 2,)),
        ],
        compiler_params=pltpu.CompilerParams(vmem_limit_bytes=4 << 20),
        name="pack",
    )(scored, *pinned(keys, values, queries))
    first = [sent] + [shifted(sent, 0, 0, -2 * k) for k in range(1, n_outer)]
    held = gathered(first, tok)
    places = [place for _, at in held for place in at]
    dx, dy, dz, upper = zip(*places)
    pairs = pair_at(dx, dy, dz)
    table = jnp.where(np.asarray(upper) == 1, 2 * n_ctx - 1 - pairs, pairs)
    mine = lax.dynamic_index_in_dim(pair_of, ctx, 0, False)
    group_pairs = pair_at([0] * n_outer, [0] * n_outer, EVEN)[:, None]
    group_rows = jnp.stack([p[block - 16 : block - 16 + r_dev, 0] for p in first])
    group_rows = group_rows.astype(jnp.int32)
    position = jnp.where(
        group_rows < half,
        group_pairs * half + group_rows,
        (2 * n_ctx - 1 - group_pairs) * half + group_rows - half,
    ).reshape(tokens)
    position = jnp.repeat(position, heads // 2)[:, None]
    meta = jnp.stack([mine, 2 * n_ctx - 1 - mine, doc_start[0]]).astype(jnp.int32)

    selected, k_sorted, v_sorted = pl.pallas_call(
        functools.partial(scored_kernel, n_outer),
        out_shape=[
            jax.ShapeDtypeStruct((tokens * heads // 2, 2 * HD), jnp.bfloat16),
            pltpu.HBM((seq, HD), jnp.bfloat16),
            pltpu.HBM((seq, HD), jnp.bfloat16),
        ],
        in_specs=[smem] * 2 + [vmem] * (1 + n_outer + len(held)),
        out_specs=[vmem, hbm, hbm],
        scratch_shapes=[
            pltpu.VMEM((seq, HD), jnp.bfloat16),
            pltpu.VMEM((seq, HD), jnp.bfloat16),
            pltpu.VMEM((tokens * heads, seq), jnp.float32),
            pltpu.SemaphoreType.DMA((2,)),
        ],
        compiler_params=pltpu.CompilerParams(vmem_limit_bytes=24 << 20),
        cost_estimate=pl.CostEstimate(
            flops=4 * tokens * heads * HD * seq, bytes_accessed=4 << 20, transcendentals=0
        ),
        name="scored_attention",
    )(table, meta, position, *first, *[array for array, _ in held])
    selected = selected.reshape(tokens, heads * HD)

    every = inner_spread(jnp.tile(selected, (BIG, 1)))
    partial = pl.pallas_call(
        project_kernel,
        out_shape=jax.ShapeDtypeStruct((n_ctx * r_dev, out_weight.shape[1]), jnp.bfloat16),
        in_specs=[vmem] * 2,
        out_specs=vmem,
        compiler_params=pltpu.CompilerParams(vmem_limit_bytes=8 << 20),
        name="out_projection",
    )(every, out_weight)
    steps = pl.cdiv(vocab, HEAD_TILE)
    wide = steps * HEAD_TILE
    width = out_weight.shape[1]
    partial, late_weight = lax.optimization_barrier((partial, head_weight.T))
    parts = tp_parts(partial)
    held_weight = pl.pallas_call(
        load_kernel,
        out_shape=jax.ShapeDtypeStruct((wide, width), jnp.bfloat16),
        in_specs=[hbm],
        out_specs=vmem,
        scratch_shapes=[pltpu.SemaphoreType.DMA((steps,))],
        compiler_params=pltpu.CompilerParams(vmem_limit_bytes=12 << 20),
        cost_estimate=pl.CostEstimate(
            flops=0, bytes_accessed=4 * wide * width, transcendentals=0
        ),
        name="load_head",
    )(*pinned(late_weight))
    held_weight, parts = lax.optimization_barrier((held_weight, parts))

    rows = n_ctx * r_dev
    residual = owned(residual_rows.reshape(n_outer, BIG, r_dev, width)).transpose(1, 0, 2, 3)
    residual = residual.reshape(rows, width)

    orders = row_orders(r_dev)

    def source(order):
        dx, dy, dz, j = [np.asarray(d, np.int32) for d in zip(*[row for rows in order for row in rows])]
        there = (z + dz) % NZ
        place = (there % 2 * NY + (y + dy) % NY) * NX + (x + dx) % NX
        return place * tokens + (there // 2 - z // 2) % n_outer * r_dev + j

    outs = [
        jax.ShapeDtypeStruct((len(rows_of), wide // 2), jnp.bfloat16)
        for order in orders
        for rows_of in order
    ]
    sums = pl.pallas_call(
        functools.partial(head_kernel, vocab),
        out_shape=outs,
        in_specs=[vmem] * 8,
        out_specs=[vmem] * len(outs),
        compiler_params=pltpu.CompilerParams(vmem_limit_bytes=20 << 20),
        name="head",
    )(
        *parts,
        residual,
        norm_gain.reshape(1, width),
        jnp.stack([source(order) for order in orders], axis=1),
        held_weight,
    )
    (p_keep, p_up, p_down), (q_keep, q_up, q_down) = orders
    even_rows = [row for row in p_keep if row[2] in EVEN]
    n_even = len(even_rows)
    n_sent = n_even // 2

    def attention(side, queries, whole):
        part = heads // 2
        return pl.pallas_call(
            functools.partial(main_kernel, side),
            out_shape=jax.ShapeDtypeStruct((tok, heads * HD), jnp.bfloat16),
            in_specs=[smem, vmem] + [hbm] * (2 + len(whole)),
            out_specs=hbm,
            scratch_shapes=[
                pltpu.VMEM((tok, part * HD), jnp.bfloat16),
                pltpu.VMEM((seq, HD), jnp.bfloat16),
                pltpu.VMEM((seq, HD), jnp.bfloat16),
                pltpu.VMEM((part * half, 2 * HD), jnp.bfloat16),
                pltpu.VMEM((part * half, HD), jnp.float32),
                pltpu.VMEM((part * half, 2 * HD), jnp.float32),
                pltpu.SemaphoreType.DMA((5,)),
            ],
            input_output_aliases={4: 0} if whole else {},
            compiler_params=pltpu.CompilerParams(vmem_limit_bytes=20 << 20),
            cost_estimate=pl.CostEstimate(
                flops=4 * tok * heads * HD * seq, bytes_accessed=4 << 20, transcendentals=0
            ),
            name="attention",
        )(meta, queries, *pinned(k_sorted, v_sorted), *whole)

    kept, late_queries = lax.optimization_barrier((sums[0], queries))
    p = [kept, shifted(sums[1], 1, 0, 0), shifted(sums[2], -1, 0, 0)]
    q = [sums[3], shifted(sums[4], 0, 0, 1), shifted(sums[5], 0, 0, -1)]
    attended = attention(0, late_queries, [])
    attended, p, q = lax.optimization_barrier((attended, p, q))
    matrices = [adding(p_keep, *orders[0], "x"), adding(q_keep, *orders[1], "z")]
    sums = added(matrices, [p, q], [n_even, n_sent, n_sent], False, "add_one")
    p = [sums[0], shifted(sums[1], 0, 0, 1), shifted(sums[2], 0, 0, -1)]
    q = [sums[3], shifted(sums[4], 1, 0, 0), shifted(sums[5], -1, 0, 0)]
    cut = lambda rows_of: (rows_of[:n_even], rows_of[n_even : n_even + n_sent], rows_of[n_even + n_sent :])
    last = [(dx, dy, dz, j) for dx, dy in NEAR for dz in EVEN for j in range(r_dev)]
    matrices = [adding(last, *cut(p_keep), "z"), adding(last, *cut(q_keep), "x")]
    sums = added(matrices, [p, q], [tokens] * len(NEAR), True, "add_two")

    nearest, late_queries = lax.optimization_barrier((sums[0], queries))
    near = [nearest] + [shifted(sums[i], *NEAR[i], 0) for i in range(1, len(NEAR))]
    attended = attention(1, late_queries, [attended])
    attended, *near = lax.optimization_barrier((attended, *near))

    def total(blocks):
        blocks = [block.astype(jnp.float32) for block in blocks]
        return (blocks[0] + blocks[1]) + (blocks[2] + blocks[3])

    sent = total(near).astype(jnp.bfloat16)
    sent = [sent[k * r_dev : (k + 1) * r_dev] for k in range(n_outer)]
    own = total([sent[0]] + [shifted(sent[k], 0, 0, 2 * k) for k in range(1, n_outer)])
    squares = own[:, vocab] + own[:, vocab + 1]
    inverse = lax.rsqrt(squares / D + EPS)
    ids = jnp.arange(wide, dtype=jnp.int32)[None, :]
    logits = jnp.where(ids < vocab, own * inverse[:, None], NEG)
    peak = jnp.max(logits, axis=1)
    mass = jnp.sum(jnp.exp(logits - peak[:, None]), axis=1)
    hit = (ids < vocab) & (ids + tp * vocab == targets[:, None])
    picked = jnp.sum(jnp.where(hit, logits, 0.0), axis=1)
    stats = jnp.stack(tp_parts(jnp.stack([peak, mass, picked])))
    joint = jnp.max(stats[:, 0], axis=0)
    joint_mass = jnp.sum(stats[:, 1] * jnp.exp(stats[:, 0] - joint[None, :]), axis=0)
    log_prob = jnp.sum(stats[:, 2], axis=0) - (joint + jnp.log(joint_mass))
    return (attended, log_prob)


def solution(mesh):
    in_specs = (
        P("ctx", "tp"),
        P("ctx", "tp"),
        P("ctx", "tp"),
        P(),
        P(),
        P("ctx"),
        P("ctx"),
        P(None, "ctx"),
        P("tp", "ctx"),
        P("ctx"),
        P("ctx", "tp"),
    )
    out_specs = (P("ctx", "tp"), P("ctx"))
    return jax.shard_map(local, mesh=mesh, in_specs=in_specs, out_specs=out_specs, check_vma=False)
```
